32 devices in a mesh: dp: 2 (over x), expert: 16 (over z, y, core).
Axes of the slice: x: 2, y: 2, z: 4, core: 2. Of those that a mesh axis runs over, the one named last changes fastest.
Arguments:
- tokens: bfloat16 [1024, 3584], P('expert'), may hold values from -6 to 6
- routes: int32 [1024, 8], P('expert'), may hold values from 0 to 31, all different within a row; in each aligned block of 64 rows (0 to 63, 64 to 127, ...) at most 24 rows name the same one
- gate_quant: int32 [1024, 8], P('expert'), may hold values from 1 to 65535
- swap_codes: int32 [8], replicated, may hold values from 0 to 4
- expert_gate_up: bfloat16 [32, 2, 3584, 1024], P('expert', None, None, 'dp'), may hold values from -0.09375 to 0.09375
- expert_down: bfloat16 [32, 1024, 3584], P('expert', 'dp'), may hold values from -0.1875 to 0.1875
- shared_gate_up: bfloat16 [1024, 2, 3584], P(('dp', 'expert')), may hold values from -0.09375 to 0.09375
- shared_down: bfloat16 [1024, 3584], P(('dp', 'expert')), may hold values from -0.1875 to 0.1875
Outputs:
- layer_out: bfloat16 [1024, 3584], P('expert', 'dp')
The draws below stay inside these ranges and needn't reach their ends.
Inputs may be any that keep to these rules, and one draw needn't show every extreme that they name: `routes`: in each aligned block of 64 rows (the rows of one index of expert) no slot id is named by more than 24 rows, a bound that some block reaches.
All inputs are finite; a program needn't handle non-finite values.
Results may differ from the reference program's by a relative error of at most 0.007.
Values may be sent and summed in bfloat16 or wider, within the bound.
No kernel may reach another device: no remote copies, remote signals or barrier semaphores. Data moves between devices by JAX's collectives and lax.ppermute only.
A program may use at most 192 MiB of HBM per device.

```python
import math
import jax
import jax.numpy as jnp
import numpy as np
from jax import lax

D = 3584
HID = 1024
SH = 1024
TOP = 8
EXP_DEV = 2
TOK_DEV = 64
EXPERTS = 32
MOST = 24
TOKENS = 1024
N_DP = 2
N_EXPERT = 16


def with_ends(values, key, least, top_value):
    extent = values.shape
    place = [jax.random.randint(jax.random.fold_in(key, axis), (), 0, extent[axis]) for axis in range(len(extent))]
    values = values.at[tuple(place)].set(least)
    longest = extent.index(max(extent))
    place[longest] = (place[longest] + 1) % extent[longest]
    return values.at[tuple(place)].set(top_value)


def level_of(stream_key, dims, split, least, top_value):
    loudness = 1.0
    for dim, blocks in split:
        draws = jax.random.uniform(jax.random.fold_in(jax.random.fold_in(stream_key, 6), dim), (blocks,), jnp.float32, least / len(split), top_value / len(split))
        loudness = loudness * jnp.repeat(jnp.exp(draws), dims[dim] // blocks).reshape((-1,) + (1,) * (len(dims) - 1 - dim))
    return loudness


def deal_out(own_key, own, number, rows, number_of, top, most, skew):
    sequence = jax.random.permutation(own_key, number_of)
    packed, common = load_shares(number_of, rows * top, most, skew, True), load_shares(number_of, rows * top, most, skew, False)
    places = jnp.arange(number_of)

    def named(lengths, turn):
        used = int((lengths > 0).sum())
        fixed = max(1, used // 4)
        moved = fixed + (places - fixed + turn * (used - fixed)) % max(1, number_of - fixed)
        return jnp.zeros((number_of,), jnp.int32).at[sequence[jnp.where(places < fixed, places, moved)]].set(jnp.asarray(lengths, jnp.int32))

    lengths = jnp.where(number % 4 == 0, named(packed, number // 4), named(common, number - number // 4 - 1))
    mixed = jax.random.permutation(jax.random.fold_in(own, 3), number_of)
    source_of, receiver = mixed[0:number_of // 2 * 2:2], mixed[1:number_of // 2 * 2:2]
    margin = jnp.minimum(lengths[source_of] - 1, most - lengths[receiver]) // 2
    margin = jnp.where((source_of == sequence[0]) | (receiver == sequence[0]) | (lengths[receiver] == 0), 0, jnp.maximum(margin, 0))
    moved = jax.random.randint(jax.random.fold_in(own, 4), (number_of // 2,), 0, 1 << 20) % (margin + 1)
    lengths = lengths.at[source_of].add(-moved).at[receiver].add(moved)
    items = jnp.searchsorted(jnp.cumsum(lengths), jnp.arange(rows * top), side="right").astype(jnp.int32)
    grid = items.reshape(top, rows).T
    grid = grid[jax.random.permutation(jax.random.fold_in(own, 1), rows)]
    turn = jax.random.randint(jax.random.fold_in(own, 2), (rows, 1), 0, top)
    return jnp.take_along_axis(grid, (jnp.arange(top)[None, :] + turn) % top, axis=1)


def load_shares(number_of, total, bound, slope, full):
    weights = [(1 << 20) // math.isqrt(grade ** slope) + 1 for grade in range(1, number_of + 1)]
    largest = bound if full else min(bound, max(-(-total // number_of), total * weights[0] // sum(weights)))
    least = 1 if total - largest >= number_of - 1 else 0
    given, spare = [largest] + [least] * (number_of - 1), total - largest - least * (number_of - 1)
    while spare > 0:
        movable = [i for i in range(1, number_of) if given[i] < largest] or [i for i in range(1, number_of) if given[i] < bound]
        mass, left = sum([weights[i] for i in movable]), spare
        for i in movable:
            extra = min(bound - given[i], max(1, left * weights[i] // mass), spare)
            given[i] = given[i] + extra
            spare = spare - extra
    return np.array(given)


def centred(own_key, shape, spread, most, shards=(), kind=jnp.bfloat16):
    gain = level_of(own_key, shape, shards, -0.22, 0.18) if shards else 1.0
    values = jax.random.normal(own_key, shape, jnp.float32) * spread * gain
    return jnp.minimum(jnp.maximum(values, -most), most).astype(kind)


def setup_inputs(seed: int = 0) -> dict:
    key_list = jax.random.split(jax.random.key(seed), 9)
    tokens = centred(key_list[0], (TOKENS, D), 1.0, 6.0, ((0, 16),))
    routes_keys = jax.random.split(jax.random.fold_in(key_list[1], 1), TOKENS // TOK_DEV)
    routes_turns = jax.random.permutation(jax.random.fold_in(key_list[1], 3), TOKENS // TOK_DEV)
    routes = jax.vmap(lambda own, number: deal_out(jax.random.fold_in(key_list[1], 2), own, number, TOK_DEV, EXPERTS, TOP, MOST, 2))(routes_keys, routes_turns).reshape((TOKENS, TOP))
    gate_quant = with_ends(jax.random.randint(key_list[2], (TOKENS, TOP), 1, 65536), jax.random.fold_in(key_list[2], 1), 1, 65535).astype(jnp.int32)
    swap_codes = with_ends(jax.random.randint(key_list[3], (N_EXPERT // 2,), 0, EXP_DEV * EXP_DEV + 1), jax.random.fold_in(key_list[3], 1), 0, EXP_DEV * EXP_DEV).astype(jnp.int32)
    expert_gate_up = centred(key_list[4], (EXPERTS, 2, D, HID), D ** -0.5, 0.09375, ((0, 16), (3, 2)))
    expert_down = centred(key_list[5], (EXPERTS, HID, D), HID ** -0.5, 0.1875, ((0, 16), (1, 2)))
    shared_gate_up = centred(key_list[6], (SH, 2, D), D ** -0.5, 0.09375, ((0, 32),))
    shared_down = centred(key_list[7], (SH, D), SH ** -0.5, 0.1875, ((0, 32),))
    return dict(tokens=tokens, routes=routes, gate_quant=gate_quant, swap_codes=swap_codes, expert_gate_up=expert_gate_up, expert_down=expert_down, shared_gate_up=shared_gate_up, shared_down=shared_down)


routed_scale = 2.5


def remap_table(swap_codes, experts, per_device, half_width):
    expert_ids = jnp.arange(experts, dtype=jnp.int32)
    holder = expert_ids // per_device
    slot_index = expert_ids % per_device
    pair_ids = jnp.arange(half_width, dtype=jnp.int32)
    pair_code = jnp.sum(jnp.where((holder % half_width)[:, None] == pair_ids[None, :], swap_codes[None, :], 0), axis=1).astype(jnp.int32)
    active = pair_code > 0
    lower = holder < half_width
    low_slot = (pair_code - 1) // per_device
    high_slot = (pair_code - 1) % per_device
    from_low = active & lower & (slot_index == low_slot)
    from_high = active & jnp.logical_not(lower) & (slot_index == high_slot)
    return jnp.where(from_low, (holder + half_width) * per_device + high_slot, jnp.where(from_high, (holder - half_width) * per_device + low_slot, expert_ids)).astype(jnp.int32)


def reference(tokens, routes, gate_quant, swap_codes, expert_gate_up, expert_down, shared_gate_up, shared_down):
    block_rows = 128
    remapped = remap_table(swap_codes, EXPERTS, EXP_DEV, N_EXPERT // 2)
    flat_target = jnp.take(remapped, routes.reshape(-1), axis=0).astype(jnp.int32)
    quant_float = gate_quant.astype(jnp.float32)
    gate_weights = (routed_scale * quant_float / jnp.sum(quant_float, axis=1, keepdims=True)).reshape(-1)
    sorted_ids = jnp.argsort(flat_target, stable=True).astype(jnp.int32)
    counts = jnp.zeros((EXPERTS,), jnp.int32).at[flat_target].add(1)
    starts = (jnp.cumsum(counts) - counts).astype(jnp.int32)
    padded_ids = jnp.concatenate([sorted_ids, jnp.zeros((block_rows,), jnp.int32)])
    quarter = HID // N_DP

    def one_expert(expert, running):
        gate_up = expert_gate_up[expert]
        down = expert_down[expert]

        def more(state):
            return state[0] * block_rows < counts[expert]

        def step(state):
            block_no, accum = state
            begin = (starts[expert] + block_no * block_rows).astype(jnp.int32)
            picked = lax.dynamic_slice_in_dim(padded_ids, begin, block_rows)
            is_live = (block_no * block_rows + jnp.arange(block_rows, dtype=jnp.int32)) < counts[expert]
            rows = jnp.take(tokens, picked // TOP, axis=0)
            gate_part = jnp.dot(rows, gate_up[0], preferred_element_type=jnp.float32)
            up_part = jnp.dot(rows, gate_up[1], preferred_element_type=jnp.float32)
            activated = (jax.nn.silu(gate_part) * up_part).astype(jnp.bfloat16)
            output = jnp.zeros((block_rows, D), jnp.float32)
            for quarter_no in range(N_DP):
                piece = jnp.dot(activated[:, quarter_no * quarter:(quarter_no + 1) * quarter], down[quarter_no * quarter:(quarter_no + 1) * quarter], preferred_element_type=jnp.float32).astype(jnp.bfloat16)
                output = output + lax.optimization_barrier(piece).astype(jnp.float32)
            weight = jnp.where(is_live, jnp.take(gate_weights, picked), jnp.zeros_like(gate_weights[:block_rows]))
            accum = accum.at[picked // TOP].add(weight[:, None] * output)
            return block_no + 1, accum

        return lax.while_loop(more, step, (jnp.int32(0), running))[1]

    routed = lax.fori_loop(0, EXPERTS, one_expert, jnp.zeros((TOKENS, D), jnp.float32))
    shared_gate = jnp.dot(tokens, shared_gate_up[:, 0, :].T, preferred_element_type=jnp.float32)
    shared_up = jnp.dot(tokens, shared_gate_up[:, 1, :].T, preferred_element_type=jnp.float32)
    shared_act = (jax.nn.silu(shared_gate) * shared_up).astype(jnp.bfloat16)
    shared_out = jnp.dot(shared_act, shared_down, preferred_element_type=jnp.float32)
    return (routed + shared_out).astype(jnp.bfloat16)
```

```python
import jax
import jax.numpy as jnp
from jax import lax
from jax.sharding import PartitionSpec as P

routed_scale = 2.5


def remapped(routes, swap_codes, per_device, half_width):
    owner = routes // per_device
    slot = routes % per_device
    pair_ids = jnp.arange(half_width, dtype=jnp.int32)
    code = jnp.sum(
        jnp.where((owner % half_width)[..., None] == pair_ids, swap_codes, 0), axis=-1
    )
    lower = owner < half_width
    low_slot = (code - 1) // per_device
    high_slot = (code - 1) % per_device
    traded = (code > 0) & (slot == jnp.where(lower, low_slot, high_slot))
    partner = jnp.where(
        lower,
        (owner + half_width) * per_device + high_slot,
        (owner - half_width) * per_device + low_slot,
    )
    return jnp.where(traded, partner, routes)


def local(
    tokens, routes, gate_quant, swap_codes, expert_gate_up, expert_down, shared_gate_up, shared_down
):
    axis_width = lax.axis_size("expert")
    half_width = axis_width // 2
    per_device = expert_down.shape[0]
    tok_rows = tokens.shape[0]
    model_dim = tokens.shape[1]
    top_count = routes.shape[1]
    experts = per_device * axis_width
    capacity = 3 * tok_rows * top_count // (2 * experts)
    expert_ids = jnp.arange(experts, dtype=jnp.int32)
    rows_gate_up = lax.all_gather(shared_gate_up, "expert", axis=0, tiled=True)
    rows_down = lax.all_gather(shared_down, "expert", axis=0, tiled=True)
    projected = jnp.einsum("td,rgd->gtr", tokens, rows_gate_up, preferred_element_type=jnp.float32)
    activated = (jax.nn.silu(projected[0]) * projected[1]).astype(jnp.bfloat16)
    shared_part = jnp.dot(activated, rows_down, preferred_element_type=jnp.float32)
    flat_target = remapped(routes, swap_codes, per_device, half_width).reshape(-1)
    assign_count = flat_target.shape[0]
    onehot = (flat_target[:, None] == expert_ids[None, :]).astype(jnp.int32)
    rank_in = jnp.sum((jnp.cumsum(onehot, axis=0) - 1) * onehot, axis=1)
    slot_place = flat_target * capacity + rank_in
    source = (
        jnp.zeros((experts * capacity,), jnp.int32)
        .at[slot_place]
        .set(jnp.arange(1, assign_count + 1, dtype=jnp.int32))
    )
    filled = source > 0
    picked_rows = jnp.take(tokens, jnp.maximum(source - 1, 0) // top_count, axis=0)
    outgoing = jnp.where(filled[:, None], picked_rows, jnp.zeros_like(picked_rows))
    outgoing = outgoing.reshape(axis_width, per_device, capacity, model_dim)
    projected = jnp.einsum(
        "nemd,egdh->gnemh",
        lax.all_to_all(outgoing, "expert", split_axis=0, concat_axis=0, tiled=True),
        expert_gate_up,
        preferred_element_type=jnp.float32,
    )
    activated = (jax.nn.silu(projected[0]) * projected[1]).astype(jnp.bfloat16)
    partial_out = jnp.einsum(
        "nemh,ehd->nemd", activated, expert_down, preferred_element_type=jnp.float32
    ).astype(jnp.bfloat16)
    returned = lax.all_to_all(partial_out, "expert", split_axis=0, concat_axis=0, tiled=True)
    out_width = returned.shape[3]
    per_slot = returned.reshape(experts * capacity, out_width)
    gathered = jnp.take(per_slot, slot_place, axis=0).reshape(tok_rows, top_count, out_width)
    quant_float = gate_quant.astype(jnp.float32)
    gate_weights = routed_scale * quant_float / jnp.sum(quant_float, axis=1, keepdims=True)
    routed = jnp.einsum("tk,tkd->td", gate_weights, gathered.astype(jnp.float32))
    local_term = routed + shared_part
    total = lax.psum_scatter(local_term, "dp", scatter_dimension=1, tiled=True)
    return total.astype(jnp.bfloat16)


def solution(mesh):
    in_specs = (
        P("expert", None),
        P("expert", None),
        P("expert", None),
        P(),
        P("expert", None, None, "dp"),
        P("expert", "dp", None),
        P(("dp", "expert"), None, None),
        P(("dp", "expert"), None),
    )
    out_specs = P("expert", "dp")
    return jax.shard_map(local, mesh=mesh, in_specs=in_specs, out_specs=out_specs, check_vma=False)
```

```python
import jax
import jax.numpy as jnp
from jax import lax
from jax.sharding import PartitionSpec as P

routed_scale = 2.5
f32 = jnp.float32
bf16 = jnp.bfloat16


def remapped(routes, swap_codes, per_device, half_width):
    owner = routes // per_device
    slot = routes % per_device
    pair_ids = jnp.arange(half_width, dtype=jnp.int32)
    code = jnp.sum(
        jnp.where((owner % half_width)[..., None] == pair_ids, swap_codes, 0), axis=-1
    )
    lower = owner < half_width
    low_slot = (code - 1) // per_device
    high_slot = (code - 1) % per_device
    traded = (code > 0) & (slot == jnp.where(lower, low_slot, high_slot))
    partner = jnp.where(
        lower,
        (owner + half_width) * per_device + high_slot,
        (owner - half_width) * per_device + low_slot,
    )
    return jnp.where(traded, partner, routes)


def hop(x, by):
    return lax.ppermute(x, "expert", [(i, i ^ by) for i in range(lax.axis_size("expert"))])


def hop_x(x, by):
    return lax.ppermute(x, "dp", [(i, i ^ by) for i in range(lax.axis_size("dp"))])


def local(
    tokens, routes, gate_quant, swap_codes, expert_gate_up, expert_down, shared_gate_up, shared_down
):
    axis_width = lax.axis_size("expert")
    nx = lax.axis_size("dp")
    ny = nx
    nz = axis_width // (2 * ny)
    zs = 2 * ny
    per_device = expert_down.shape[0]
    tok_rows, model_dim = tokens.shape
    experts = per_device * axis_width
    me = lax.axis_index("expert")
    mx = lax.axis_index("dp")
    part = tok_rows // nx
    width = model_dim // nx

    target = remapped(routes, swap_codes, per_device, axis_width // 2)
    quant = gate_quant.astype(f32)
    gates = routed_scale * quant / jnp.sum(quant, axis=1, keepdims=True)
    expert_ids = jnp.arange(experts, dtype=jnp.int32)
    table = jnp.sum(jnp.where(target[:, :, None] == expert_ids, gates[:, :, None], 0.0), axis=1)
    every = lax.all_gather(table, "expert", axis=0, tiled=False)
    mine = lax.dynamic_slice_in_dim(every, me * per_device, per_device, axis=2)
    weight = jnp.take(mine, jnp.arange(axis_width) ^ me, axis=0)

    def canonical(parts):
        stacked = jnp.stack(parts)
        return jnp.take(stacked, jnp.arange(nx) ^ mx, axis=0).reshape(tok_rows, model_dim)

    own_part = lax.dynamic_slice_in_dim(tokens, mx * part, part, axis=0)
    by_z = {k: hop(own_part, k * zs) for k in range(1, nz)}
    blocks = {(0, 0): tokens}
    for j in range(1, ny):
        blocks[0, j] = hop(tokens, 2 * j)
    for k in range(1, nz):
        for j in range(ny):
            first = by_z[k] if j == 0 else hop(by_z[k], 2 * j)
            blocks[k, j] = canonical([first] + [hop_x(first, h) for h in range(1, nx)])

    sg = shared_gate_up[:, 0, :]
    su = shared_gate_up[:, 1, :]

    def layer(rows, scale):
        total = None
        for e in range(per_device):
            g = jnp.dot(rows, expert_gate_up[e, 0], preferred_element_type=f32)
            u = jnp.dot(rows, expert_gate_up[e, 1], preferred_element_type=f32)
            act = (jax.nn.silu(g) * u * scale[:, e : e + 1]).astype(bf16)
            out = jnp.dot(act, expert_down[e], preferred_element_type=f32)
            total = out if total is None else total + out
        g = lax.dot_general(rows, sg, (((1,), (1,)), ((), ())), preferred_element_type=f32)
        u = lax.dot_general(rows, su, (((1,), (1,)), ((), ())), preferred_element_type=f32)
        act = (jax.nn.silu(g) * u).astype(bf16)
        return total + jnp.dot(act, shared_down, preferred_element_type=f32)

    def feature_part(v, h):
        return lax.dynamic_slice_in_dim(v, (mx ^ h) * width, width, axis=v.ndim - 1)

    def added(own, others):
        total = own.astype(f32)
        for other in others:
            total = total + other.astype(f32)
        return total

    done = {}
    for k in range(nz):
        own_rows = jnp.concatenate([blocks[k, j] for j in range(ny)], axis=0)
        rows = jnp.concatenate([own_rows, hop(own_rows, 1)], axis=0)
        scale = weight[k * zs : (k + 1) * zs].reshape(ny, 2, tok_rows, per_device)
        scale = scale.transpose(1, 0, 2, 3).reshape(-1, per_device)
        out = layer(rows, scale)
        half = ny * tok_rows
        from_core = hop(out[half:].astype(bf16), 1)
        chip = added(out[:half], [from_core]).astype(bf16).reshape(ny, tok_rows, model_dim)
        if k % 2:
            got = [hop_x(feature_part(chip, h), h) for h in range(1, nx)]
            chip = added(feature_part(chip, 0), got).astype(bf16)
            got = [hop(chip[j], 2 * j) for j in range(1, ny)]
            plane = added(chip[0], got)
        else:
            got = [hop(chip[j], 2 * j) for j in range(1, ny)]
            chip = added(chip[0], got).astype(bf16)
            got = [hop_x(feature_part(chip, h), h) for h in range(1, nx)]
            plane = added(feature_part(chip, 0), got)
        done[k] = plane if k == 0 else hop(plane.astype(bf16), k * zs)
    return added(done[0], [done[k] for k in range(1, nz)]).astype(bf16)


def solution(mesh):
    in_specs = (
        P("expert", None),
        P("expert", None),
        P("expert", None),
        P(),
        P("expert", None, None, "dp"),
        P("expert", "dp", None),
        P(("dp", "expert"), None, None),
        P(("dp", "expert"), None),
    )
    out_specs = P("expert", "dp")
    return jax.shard_map(local, mesh=mesh, in_specs=in_specs, out_specs=out_specs, check_vma=False)
```

```python
import functools

import jax
import jax.numpy as jnp
from jax import lax
from jax.experimental import pallas as pl
from jax.experimental.pallas import tpu as pltpu
from jax.sharding import PartitionSpec as P

routed_scale = 2.5
lanes = 128
f32 = jnp.float32
bf16 = jnp.bfloat16


def remapped(routes, swap_codes, per_device, half_width):
    owner = routes // per_device
    slot = routes % per_device
    pair_ids = jnp.arange(half_width, dtype=jnp.int32)
    code = jnp.sum(
        jnp.where((owner % half_width)[..., None] == pair_ids, swap_codes, 0), axis=-1
    )
    lower = owner < half_width
    low_slot = (code - 1) // per_device
    high_slot = (code - 1) % per_device
    traded = (code > 0) & (slot == jnp.where(lower, low_slot, high_slot))
    partner = jnp.where(
        lower,
        (owner + half_width) * per_device + high_slot,
        (owner - half_width) * per_device + low_slot,
    )
    return jnp.where(traded, partner, routes)


def hop(x, by):
    return lax.ppermute(x, "expert", [(i, i ^ by) for i in range(lax.axis_size("expert"))])


def hop_x(x, by):
    return lax.ppermute(x, "dp", [(i, i ^ by) for i in range(lax.axis_size("dp"))])


def ffn_kernel(
    levels, x_first, nx, ny, tok_rows, top_count, model_dim, hid_tile, out_tile, n_units, *refs
):
    slots = refs[0]
    units = refs[1 : 1 + n_units]
    sh_gu, sh_dn, gu_own, gu_sib, dn_own, dn_sib = refs[1 + n_units : 7 + n_units]
    refs = refs[7 + n_units :]
    outs = [refs[i * nx : (i + 1) * nx] for i in range(len(levels))]
    rows_in, shared_w, wgu, wdn, act, scale, sem_x, sem_s, sem_gu, sem_dn = refs[len(levels) * nx :]
    mx = lax.axis_index("dp")
    part = tok_rows // nx
    width = model_dim // nx
    per_device, _, _, hidden = gu_own.shape
    tiles = hidden // hid_tile
    n_slots = 2 * per_device
    experts_k = n_slots * hidden
    sp = sh_dn.shape[0]

    copies = []
    at = 0
    for i, level in enumerate(levels):
        for j in range(ny):
            base = (i * ny + j) * tok_rows
            for h in range(1 if level == 0 else nx):
                if level == 0:
                    dst = rows_in.at[pl.ds(base, tok_rows)]
                else:
                    start = pl.multiple_of(base + (mx ^ h) * part, part)
                    dst = rows_in.at[pl.ds(start, part)]
                copies.append(pltpu.make_async_copy(units[at], dst, sem_x.at[at]))
                at += 1
    shared_copy = pltpu.make_async_copy(sh_gu, shared_w, sem_s.at[0])

    def gu_copy(src, e, t, i):
        return pltpu.make_async_copy(
            src.at[e, :, :, pl.ds(t * hid_tile, hid_tile)], wgu.at[i], sem_gu.at[i]
        )

    def dn_copy(src, e, h, s):
        column = pl.multiple_of((mx ^ h) * width, lanes)
        return pltpu.make_async_copy(
            src.at[e, :, pl.ds(column, width)],
            wdn.at[h, pl.ds(s * hidden, hidden)],
            sem_dn.at[h, s],
        )

    def sh_copy(h):
        column = pl.multiple_of((mx ^ h) * width, lanes)
        return pltpu.make_async_copy(
            sh_dn.at[:, pl.ds(column, width)],
            wdn.at[h, pl.ds(experts_k, sp)],
            sem_dn.at[h, n_slots],
        )

    for copy in copies:
        copy.start()
    shared_copy.start()
    for s in range(n_slots):
        src = gu_own if s < per_device else gu_sib
        for t in range(tiles):
            gu_copy(src, s % per_device, t, s * tiles + t).start()
    order = list(range(1, nx)) + [0]
    dn_waits = {h: [] for h in order}
    for h in order:
        for s in range(n_slots):
            src = dn_own if s < per_device else dn_sib
            dn_waits[h].append(dn_copy(src, s % per_device, h, s))
        dn_waits[h].append(sh_copy(h))
        for copy in dn_waits[h]:
            copy.start()

    for copy in copies:
        copy.wait()
    extra = rows_in[:, model_dim:].astype(f32)
    named = extra[:, :top_count]
    quant = extra[:, top_count : 2 * top_count] * 256.0 + extra[:, 2 * top_count : 3 * top_count]
    gates = routed_scale * quant / jnp.sum(quant, axis=1, keepdims=True)
    n_rows = rows_in.shape[0]
    for s in range(n_slots):
        mine = jnp.where(named == slots[s].astype(f32), gates, 0.0)
        column = jnp.sum(mine, axis=1, keepdims=True)
        scale[s] = jnp.broadcast_to(column, (n_rows, lanes))

    def silu(v):
        return v / (1.0 + jnp.exp(-v))

    shared_copy.wait()
    both = lax.dot_general(
        rows_in[:, :model_dim],
        shared_w[...],
        (((1,), (1,)), ((), ())),
        preferred_element_type=f32,
    )
    act[:, experts_k : experts_k + sp] = (silu(both[:, :sp]) * both[:, sp:]).astype(bf16)

    @pl.loop(0, n_slots * tiles)
    def _(i):
        pltpu.make_async_copy(
            gu_own.at[0, :, :, pl.ds(0, hid_tile)], wgu.at[i], sem_gu.at[i]
        ).wait()
        g = jnp.dot(rows_in[:, :model_dim], wgu[i, 0], preferred_element_type=f32)
        u = jnp.dot(rows_in[:, :model_dim], wgu[i, 1], preferred_element_type=f32)
        by = scale[i // tiles]
        by = jnp.concatenate([by] * (hid_tile // lanes), axis=1)
        column = pl.multiple_of(i * hid_tile, hid_tile)
        act[:, pl.ds(column, hid_tile)] = (silu(g) * u * by).astype(bf16)

    level_rows = ny * tok_rows
    for h in order:
        for copy in dn_waits[h]:
            copy.wait()

        @pl.loop(0, width // out_tile)
        def _(n):
            column = pl.multiple_of(n * out_tile, out_tile)
            value = jnp.dot(
                act[...], wdn[h, :, pl.ds(column, out_tile)], preferred_element_type=f32
            ).astype(bf16)
            for i in range(len(levels)):
                if x_first[i]:
                    outs[i][h][:, pl.ds(column, out_tile)] = value[
                        i * level_rows : (i + 1) * level_rows
                    ]
                else:
                    for j in range(ny):
                        base = i * level_rows + j * tok_rows
                        outs[i][j][h, :, pl.ds(column, out_tile)] = value[base : base + tok_rows]


def local(
    tokens, routes, gate_quant, swap_codes, expert_gate_up, expert_down, shared_gate_up, shared_down
):
    axis_width = lax.axis_size("expert")
    nx = lax.axis_size("dp")
    ny = nx
    nz = axis_width // (2 * ny)
    zs = 2 * ny
    per_device, hidden, model_dim = expert_down.shape
    tok_rows = tokens.shape[0]
    top_count = routes.shape[1]
    me = lax.axis_index("expert")
    mx = lax.axis_index("dp")
    part = tok_rows // nx
    width = model_dim // nx
    hid_tile = 256 if hidden % 256 == 0 else 128
    out_tile = 256 if width % 256 == 0 else 128

    pad = -3 * top_count % lanes
    wide = jnp.concatenate(
        [
            tokens,
            routes.astype(bf16),
            (gate_quant // 256).astype(bf16),
            (gate_quant % 256).astype(bf16),
            jnp.zeros((tok_rows, pad), bf16),
        ],
        axis=1,
    )
    wide_dim = wide.shape[1]

    gu_sib = hop(expert_gate_up, 1)
    dn_sib = hop(expert_down, 1)
    shared_rows = shared_down.shape[0]
    shared_own = jnp.concatenate(
        [shared_gate_up[:, 0, :], shared_gate_up[:, 1, :], shared_down], axis=0
    )
    shared_both = jnp.stack([shared_own, hop(shared_own, 1)])
    shared_both = shared_both.reshape(2, 3, shared_rows, model_dim).transpose(1, 0, 2, 3)
    shared_both = shared_both.reshape(3, 2 * shared_rows, model_dim)
    shared_both = jnp.pad(shared_both, ((0, 0), (0, -2 * shared_rows % 16), (0, 0)))
    sp = shared_both.shape[1]
    sh_gu = shared_both[:2].reshape(2 * sp, model_dim)
    sh_dn = shared_both[2]

    my_experts = jnp.concatenate(
        [owner * per_device + jnp.arange(per_device, dtype=jnp.int32) for owner in (me, me ^ 1)]
    )
    slots = remapped(my_experts, swap_codes, per_device, axis_width // 2)

    own_part = lax.dynamic_slice_in_dim(wide, mx * part, part, axis=0)
    units = {(0, 0): [wide]}
    for j in range(1, ny):
        units[0, j] = [hop(wide, 2 * j)]
    for k in range(1, nz):
        from_z = hop(own_part, k * zs)
        for j in range(ny):
            first = from_z if j == 0 else hop(from_z, 2 * j)
            units[k, j] = [first] + [hop_x(first, h) for h in range(1, nx)]

    def added(own, others):
        total = own.astype(f32)
        for other in others:
            total = total + other.astype(f32)
        return total

    done = {}
    n_slots = 2 * per_device
    tiles = hidden // hid_tile
    half = nz // 2
    for levels in (list(range(half)), list(range(half, nz))):
        x_first = [k % 2 == 1 for k in levels]
        chunk = [u for k in levels for j in range(ny) for u in units[k, j]]
        n_rows = len(levels) * ny * tok_rows
        out_shape = []
        for first in x_first:
            shape = (ny * tok_rows, width) if first else (nx, tok_rows, width)
            out_shape += [jax.ShapeDtypeStruct(shape, bf16)] * nx
        k_total = n_slots * hidden + sp
        flops = 2 * n_rows * model_dim * (3 * n_slots * hidden + 3 * sp)
        outs = pl.pallas_call(
            functools.partial(
                ffn_kernel,
                levels,
                x_first,
                nx,
                ny,
                tok_rows,
                top_count,
                model_dim,
                hid_tile,
                out_tile,
                len(chunk),
            ),
            out_shape=out_shape,
            in_specs=[pl.BlockSpec(memory_space=pltpu.SMEM)]
            + [pl.BlockSpec(memory_space=pl.ANY)] * (len(chunk) + 6),
            out_specs=[pl.BlockSpec(memory_space=pltpu.VMEM)] * len(out_shape),
            scratch_shapes=[
                pltpu.VMEM((n_rows, wide_dim), bf16),
                pltpu.VMEM((2 * sp, model_dim), bf16),
                pltpu.VMEM((n_slots * tiles, 2, model_dim, hid_tile), bf16),
                pltpu.VMEM((nx, k_total, width), bf16),
                pltpu.VMEM((n_rows, k_total), bf16),
                pltpu.VMEM((n_slots, n_rows, lanes), f32),
                pltpu.SemaphoreType.DMA((len(chunk),)),
                pltpu.SemaphoreType.DMA((1,)),
                pltpu.SemaphoreType.DMA((n_slots * tiles,)),
                pltpu.SemaphoreType.DMA((nx, n_slots + 1)),
            ],
            compiler_params=pltpu.CompilerParams(vmem_limit_bytes=60 * 1024 * 1024),
            cost_estimate=pl.CostEstimate(
                flops=flops,
                bytes_accessed=3 * 2 * n_slots * hidden * model_dim + 6 * n_rows * model_dim,
                transcendentals=0,
            ),
        )(slots, *chunk, sh_gu, sh_dn, expert_gate_up, gu_sib, expert_down, dn_sib)
        for i, k in enumerate(levels):
            sent = outs[i * nx : (i + 1) * nx]
            if x_first[i]:
                got = [hop_x(sent[h], h) for h in range(1, nx)]
                row = added(sent[0], got).astype(bf16).reshape(ny, tok_rows, width)
                got = [hop(row[j], 2 * j) for j in range(1, ny)]
            else:
                got = [hop(sent[j], 2 * j) for j in range(1, ny)]
                row = added(sent[0], got).astype(bf16)
                got = [hop_x(row[h], h) for h in range(1, nx)]
            plane = added(row[0], got)
            done[k] = plane if k == 0 else hop(plane.astype(bf16), k * zs)
    return added(done[0], [done[k] for k in range(1, nz)]).astype(bf16)


def solution(mesh):
    in_specs = (
        P("expert", None),
        P("expert", None),
        P("expert", None),
        P(),
        P("expert", None, None, "dp"),
        P("expert", "dp", None),
        P(("dp", "expert"), None, None),
        P(("dp", "expert"), None),
    )
    out_specs = P("expert", "dp")
    return jax.shard_map(local, mesh=mesh, in_specs=in_specs, out_specs=out_specs, check_vma=False)
```

```python
import functools

import jax
import jax.numpy as jnp
from jax import lax
from jax.experimental import pallas as pl
from jax.experimental.pallas import tpu as pltpu
from jax.sharding import PartitionSpec as P

routed_scale = 2.5
lanes = 128
in_flight = 6
cut = 2048
f32 = jnp.float32
bf16 = jnp.bfloat16


def remapped(routes, swap_codes, per_device, half_width):
    owner = routes // per_device
    slot = routes % per_device
    pair_ids = jnp.arange(half_width, dtype=jnp.int32)
    code = jnp.sum(
        jnp.where((owner % half_width)[..., None] == pair_ids, swap_codes, 0), axis=-1
    )
    lower = owner < half_width
    low_slot = (code - 1) // per_device
    high_slot = (code - 1) % per_device
    traded = (code > 0) & (slot == jnp.where(lower, low_slot, high_slot))
    partner = jnp.where(
        lower,
        (owner + half_width) * per_device + high_slot,
        (owner - half_width) * per_device + low_slot,
    )
    return jnp.where(traded, partner, routes)


def hop(x, by, by_x=0):
    ne = lax.axis_size("expert")
    count = ne * lax.axis_size("dp")
    return lax.ppermute(x, ("dp", "expert"), [(i, i ^ (by_x * ne + by)) for i in range(count)])


def ffn_kernel(
    levels, x_first, nx, ny, tok_rows, top_count, model_dim, hid_tile, n_units, n_after, *refs
):
    slots = refs[0]
    units = refs[1 : 1 + n_units]
    sh_gu, sh_dn, gu_own, gu_sib, dn_own, dn_sib = refs[1 + n_units : 7 + n_units]
    refs = refs[7 + n_units + n_after :]
    outs = [refs[i * nx : (i + 1) * nx] for i in range(len(levels))]
    rows_in, shared_w, wgu, wdn, act, scale, sem_x, sem_s, sem_gu, sem_dn = refs[len(levels) * nx :]
    mx = lax.axis_index("dp")
    part = tok_rows // nx
    width = model_dim // nx
    per_device, _, _, hidden = gu_own.shape
    tiles = hidden // hid_tile
    n_slots = 2 * per_device
    experts_k = n_slots * hidden
    sp = sh_dn.shape[0]

    copies = []

    def take(unit, start, size, row):
        dst = rows_in.at[pl.ds(row, size)]
        copies.append(
            pltpu.make_async_copy(unit.at[pl.ds(start, size)], dst, sem_x.at[len(copies)])
        )

    at = 0
    for j in range(ny):
        if levels[0] == 0:
            take(units[at], 0, tok_rows, j * tok_rows)
            at += 1
        for h in range(nx):
            for n, i in enumerate(i for i in range(len(levels)) if levels[i]):
                row = (i * ny + j) * tok_rows + (mx ^ h) * part
                take(units[at], n * part, part, pl.multiple_of(row, part))
            at += 1
    shared_copy = pltpu.make_async_copy(sh_gu, shared_w, sem_s.at[0])

    def gu_copy(src, e, t, i, g):
        return pltpu.make_async_copy(
            src.at[e, g, :, pl.ds(t * hid_tile, hid_tile)], wgu.at[i, g], sem_gu.at[i, g]
        )

    cuts = [(at, min(cut, width - at)) for at in range(0, width, cut)]

    def dn_copy(src, e, h, s, n):
        at, size = cuts[n]
        column = pl.multiple_of((mx ^ h) * width + at, lanes)
        return pltpu.make_async_copy(
            src.at[e, :, pl.ds(column, size)],
            wdn.at[h, pl.ds(s * hidden, hidden), pl.ds(at, size)],
            sem_dn.at[h, n, s],
        )

    def sh_copy(h, n):
        at, size = cuts[n]
        column = pl.multiple_of((mx ^ h) * width + at, lanes)
        return pltpu.make_async_copy(
            sh_dn.at[:, pl.ds(column, size)],
            wdn.at[h, pl.ds(experts_k, sp), pl.ds(at, size)],
            sem_dn.at[h, n, n_slots],
        )

    order = list(range(1, nx)) + [0]
    gu_copies = []
    for s in range(n_slots):
        src = gu_own if s < per_device else gu_sib
        for t in range(tiles):
            for g in range(2):
                gu_copies.append(gu_copy(src, s % per_device, t, s * tiles + t, g))
    dn_copies = []
    for h in order:
        for n in range(len(cuts)):
            group = [sh_copy(h, n)]
            for s in range(n_slots):
                src = dn_own if s < per_device else dn_sib
                group.append(dn_copy(src, s % per_device, h, s, n))
            dn_copies.append((h, n, group))

    queue = gu_copies[:4] + [shared_copy] + gu_copies[4:]
    queue += [copy for _, _, group in dn_copies for copy in group]
    started = [0]

    def start_next(count):
        for copy in queue[started[0] : started[0] + count]:
            copy.start()
        started[0] += count

    def arrived(copy):
        copy.wait()
        start_next(1)

    for copy in copies:
        copy.start()
    start_next(in_flight)
    for copy in copies:
        copy.wait()
    extra = rows_in[:, model_dim:].astype(f32)
    named = extra[:, :top_count]
    quant = extra[:, top_count : 2 * top_count] * 256.0 + extra[:, 2 * top_count : 3 * top_count]
    gates = routed_scale * quant / jnp.sum(quant, axis=1, keepdims=True)
    n_rows = rows_in.shape[0]
    for s in range(n_slots):
        mine = jnp.where(named == slots[s].astype(f32), gates, 0.0)
        column = jnp.sum(mine, axis=1, keepdims=True)
        scale[s] = jnp.broadcast_to(column, (n_rows, lanes))

    def silu(v):
        return v / (1.0 + jnp.exp(-v))

    for i in range(n_slots * tiles):
        if i == 2:
            arrived(shared_copy)
            both = jnp.dot(rows_in[:, :model_dim], shared_w[...], preferred_element_type=f32)
            shared_act = (silu(both[:, :sp]) * both[:, sp:]).astype(bf16)
            act[:, experts_k : experts_k + sp] = shared_act
        for copy in gu_copies[2 * i : 2 * i + 2]:
            arrived(copy)
        g = jnp.dot(rows_in[:, :model_dim], wgu[i, 0], preferred_element_type=f32)
        u = jnp.dot(rows_in[:, :model_dim], wgu[i, 1], preferred_element_type=f32)
        by = jnp.concatenate([scale[i // tiles]] * (hid_tile // lanes), axis=1)
        act[:, i * hid_tile : (i + 1) * hid_tile] = (silu(g) * u * by).astype(bf16)

    level_rows = ny * tok_rows
    for h, n, group in dn_copies:
        for copy in group:
            arrived(copy)
        columns = pl.ds(*cuts[n])
        value = jnp.dot(act[...], wdn[h, :, columns], preferred_element_type=f32).astype(bf16)
        for i in range(len(levels)):
            if x_first[i]:
                outs[i][h][:, columns] = value[i * level_rows : (i + 1) * level_rows]
            else:
                for j in range(ny):
                    base = i * level_rows + j * tok_rows
                    outs[i][j][h, :, columns] = value[base : base + tok_rows]


def local(
    tokens, routes, gate_quant, swap_codes, expert_gate_up, expert_down, shared_gate_up, shared_down
):
    axis_width = lax.axis_size("expert")
    nx = lax.axis_size("dp")
    ny = nx
    nz = axis_width // (2 * ny)
    zs = 2 * ny
    per_device, hidden, model_dim = expert_down.shape
    tok_rows = tokens.shape[0]
    top_count = routes.shape[1]
    me = lax.axis_index("expert")
    mx = lax.axis_index("dp")
    part = tok_rows // nx
    width = model_dim // nx
    hid_tile = 256 if hidden % 256 == 0 else 128

    pad = -3 * top_count % lanes
    wide = jnp.concatenate(
        [
            tokens,
            routes.astype(bf16),
            (gate_quant // 256).astype(bf16),
            (gate_quant % 256).astype(bf16),
            jnp.zeros((tok_rows, pad), bf16),
        ],
        axis=1,
    )
    wide_dim = wide.shape[1]

    gu_sib = hop(expert_gate_up, 1)
    dn_sib = hop(expert_down, 1)
    shared_rows = shared_down.shape[0]
    shared_own = jnp.concatenate(
        [shared_gate_up[:, 0, :], shared_gate_up[:, 1, :], shared_down], axis=0
    )
    shared_both = jnp.stack([shared_own, hop(shared_own, 1)])
    shared_both = shared_both.reshape(2, 3, shared_rows, model_dim).transpose(1, 0, 2, 3)
    shared_both = shared_both.reshape(3, 2 * shared_rows, model_dim)
    shared_both = jnp.pad(shared_both, ((0, 0), (0, -2 * shared_rows % 16), (0, 0)))
    sp = shared_both.shape[1]
    sh_gu = shared_both[:2].reshape(2 * sp, model_dim).T
    sh_dn = shared_both[2]

    my_experts = jnp.concatenate(
        [owner * per_device + jnp.arange(per_device, dtype=jnp.int32) for owner in (me, me ^ 1)]
    )
    slots = remapped(my_experts, swap_codes, per_device, axis_width // 2)

    half = nz // 2
    held = lax.dynamic_slice_in_dim(wide, mx * part, part, axis=0)
    own = [wide] + [hop(wide, 2 * j) for j in range(1, ny)]
    bits = [0]
    step = half
    while step > 1:
        held = jnp.concatenate([held, hop(held, step * zs)], axis=0)
        bits = bits + [bit ^ step for bit in bits]
        step //= 2
    far = hop(held, zs)
    bits = bits + [bit ^ 1 for bit in bits]

    def spread(x):
        return [[hop(x, 2 * j, h) if j or h else x for h in range(nx)] for j in range(ny)]

    near_units = spread(held[part:])
    near = [u for j in range(ny) for u in near_units[j]]
    far = lax.optimization_barrier([far] + near)[0]
    far_units = spread(far)
    chunks = [
        [u for j in range(ny) for u in [own[j]] + near_units[j]],
        [u for j in range(ny) for u in far_units[j]],
    ]

    def added(own, others):
        total = own.astype(f32)
        for other in others:
            total = total + other.astype(f32)
        return total

    done = {}
    n_slots = 2 * per_device
    tiles = hidden // hid_tile
    after = []
    for levels in (list(range(half)), list(range(half, nz))):
        x_first = [k % 2 == 1 for k in levels]
        chunk = chunks[levels[0] // half]
        n_rows = len(levels) * ny * tok_rows
        out_shape = []
        for first in x_first:
            shape = (ny * tok_rows, width) if first else (nx, tok_rows, width)
            out_shape += [jax.ShapeDtypeStruct(shape, bf16)] * nx
        k_total = n_slots * hidden + sp
        flops = 2 * n_rows * model_dim * (3 * n_slots * hidden + 3 * sp)
        outs = pl.pallas_call(
            functools.partial(
                ffn_kernel,
                levels,
                x_first,
                nx,
                ny,
                tok_rows,
                top_count,
                model_dim,
                hid_tile,
                len(chunk),
                len(after),
            ),
            out_shape=out_shape,
            in_specs=[pl.BlockSpec(memory_space=pltpu.SMEM)]
            + [pl.BlockSpec(memory_space=pl.ANY)] * (len(chunk) + 6 + len(after)),
            out_specs=[pl.BlockSpec(memory_space=pltpu.VMEM)] * len(out_shape),
            scratch_shapes=[
                pltpu.VMEM((n_rows, wide_dim), bf16),
                pltpu.VMEM((model_dim, 2 * sp), bf16),
                pltpu.VMEM((n_slots * tiles, 2, model_dim, hid_tile), bf16),
                pltpu.VMEM((nx, k_total, width), bf16),
                pltpu.VMEM((n_rows, k_total), bf16),
                pltpu.VMEM((n_slots, n_rows, lanes), f32),
                pltpu.SemaphoreType.DMA((len(levels) * ny * nx,)),
                pltpu.SemaphoreType.DMA((1,)),
                pltpu.SemaphoreType.DMA((n_slots * tiles, 2)),
                pltpu.SemaphoreType.DMA((nx, -(-width // cut), n_slots + 1)),
            ],
            compiler_params=pltpu.CompilerParams(vmem_limit_bytes=60 * 1024 * 1024),
            cost_estimate=pl.CostEstimate(
                flops=flops,
                bytes_accessed=3 * 2 * n_slots * hidden * model_dim + 6 * n_rows * model_dim,
                transcendentals=0,
            ),
        )(slots, *chunk, sh_gu, sh_dn, expert_gate_up, gu_sib, expert_down, dn_sib, *after)
        after = outs[:1]
        for i, k in enumerate(levels):
            sent = outs[i * nx : (i + 1) * nx]
            if x_first[i]:
                got = [hop(sent[h], 0, h) for h in range(1, nx)]
                row = added(sent[0], got).astype(bf16).reshape(ny, tok_rows, width)
                got = [hop(row[j], 2 * j) for j in range(1, ny)]
            else:
                got = [hop(sent[j], 2 * j) for j in range(1, ny)]
                row = added(sent[0], got).astype(bf16)
                got = [hop(row[h], 0, h) for h in range(1, nx)]
            plane = added(row[0], got)
            done[k] = plane if k == 0 else hop(plane.astype(bf16), bits[k] * zs)
    return added(done[0], [done[k] for k in range(1, nz)]).astype(bf16)


def solution(mesh):
    in_specs = (
        P("expert", None),
        P("expert", None),
        P("expert", None),
        P(),
        P("expert", None, None, "dp"),
        P("expert", "dp", None),
        P(("dp", "expert"), None, None),
        P(("dp", "expert"), None),
    )
    out_specs = P("expert", "dp")
    return jax.shard_map(local, mesh=mesh, in_specs=in_specs, out_specs=out_specs, check_vma=False)
```

```python
import functools

import jax
import jax.numpy as jnp
from jax import lax
from jax.experimental import pallas as pl
from jax.experimental.pallas import tpu as pltpu
from jax.sharding import PartitionSpec as P

routed_scale = 2.5
lanes = 128
in_flight = 6
cut = 2048
f32 = jnp.float32
bf16 = jnp.bfloat16


def remapped(routes, swap_codes, per_device, half_width):
    owner = routes // per_device
    slot = routes % per_device
    pair_ids = jnp.arange(half_width, dtype=jnp.int32)
    code = jnp.sum(
        jnp.where((owner % half_width)[..., None] == pair_ids, swap_codes, 0), axis=-1
    )
    lower = owner < half_width
    low_slot = (code - 1) // per_device
    high_slot = (code - 1) % per_device
    traded = (code > 0) & (slot == jnp.where(lower, low_slot, high_slot))
    partner = jnp.where(
        lower,
        (owner + half_width) * per_device + high_slot,
        (owner - half_width) * per_device + low_slot,
    )
    return jnp.where(traded, partner, routes)


def hop(x, by, by_x=0):
    ne = lax.axis_size("expert")
    count = ne * lax.axis_size("dp")
    return lax.ppermute(x, ("dp", "expert"), [(i, i ^ (by_x * ne + by)) for i in range(count)])


def ffn_kernel(
    levels, x_first, nx, ny, tok_rows, top_count, model_dim, hid_tile, n_units, n_after, *refs
):
    slots = refs[0]
    units = refs[1 : 1 + n_units]
    sh_gu, sh_dn, gu_own, gu_sib, dn_own, dn_sib = refs[1 + n_units : 7 + n_units]
    refs = refs[7 + n_units + n_after :]
    groups = ny if x_first is None else len(levels)
    outs = [refs[i * nx : (i + 1) * nx] for i in range(groups)]
    rows_in, shared_w, wgu, wdn, act, scale, sem_x, sem_s, sem_gu, sem_dn = refs[groups * nx :]
    mx = lax.axis_index("dp")
    part = tok_rows // nx
    width = model_dim // nx
    per_device, _, _, hidden = gu_own.shape
    tiles = hidden // hid_tile
    n_slots = 2 * per_device
    experts_k = n_slots * hidden
    sp = sh_dn.shape[0]

    copies = []

    def take(unit, start, size, row):
        dst = rows_in.at[pl.ds(row, size)]
        copies.append(
            pltpu.make_async_copy(unit.at[pl.ds(start, size)], dst, sem_x.at[len(copies)])
        )

    at = 0
    for j in range(ny):
        if levels[0] == 0:
            take(units[at], 0, tok_rows, j * tok_rows)
            at += 1
        for h in range(nx):
            for n, i in enumerate(i for i in range(len(levels)) if levels[i]):
                row = (i * ny + j) * tok_rows + (mx ^ h) * part
                take(units[at], n * part, part, pl.multiple_of(row, part))
            at += 1
    shared_copy = pltpu.make_async_copy(sh_gu, shared_w, sem_s.at[0])

    def gu_copy(src, e, t, i, g):
        return pltpu.make_async_copy(
            src.at[e, g, :, pl.ds(t * hid_tile, hid_tile)], wgu.at[i, g], sem_gu.at[i, g]
        )

    cuts = [(at, min(cut, width - at)) for at in range(0, width, cut)]

    def dn_copy(src, e, h, s, n):
        at, size = cuts[n]
        column = pl.multiple_of((mx ^ h) * width + at, lanes)
        return pltpu.make_async_copy(
            src.at[e, :, pl.ds(column, size)],
            wdn.at[h, pl.ds(s * hidden, hidden), pl.ds(at, size)],
            sem_dn.at[h, n, s],
        )

    def sh_copy(h, n):
        at, size = cuts[n]
        column = pl.multiple_of((mx ^ h) * width + at, lanes)
        return pltpu.make_async_copy(
            sh_dn.at[:, pl.ds(column, size)],
            wdn.at[h, pl.ds(experts_k, sp), pl.ds(at, size)],
            sem_dn.at[h, n, n_slots],
        )

    order = list(range(1, nx)) + [0]
    gu_copies = []
    for s in range(n_slots):
        src = gu_own if s < per_device else gu_sib
        for t in range(tiles):
            for g in range(2):
                gu_copies.append(gu_copy(src, s % per_device, t, s * tiles + t, g))
    dn_copies = []
    for h in order:
        for n in range(len(cuts)):
            group = [sh_copy(h, n)]
            for s in range(n_slots):
                src = dn_own if s < per_device else dn_sib
                group.append(dn_copy(src, s % per_device, h, s, n))
            dn_copies.append((h, n, group))

    queue = gu_copies[:4] + [shared_copy] + gu_copies[4:]
    queue += [copy for _, _, group in dn_copies for copy in group]
    started = [0]

    def start_next(count):
        for copy in queue[started[0] : started[0] + count]:
            copy.start()
        started[0] += count

    def arrived(copy):
        copy.wait()
        start_next(1)

    for copy in copies:
        copy.start()
    start_next(in_flight)
    for copy in copies:
        copy.wait()
    extra = rows_in[:, model_dim:].astype(f32)
    named = extra[:, :top_count]
    quant = extra[:, top_count : 2 * top_count] * 256.0 + extra[:, 2 * top_count : 3 * top_count]
    gates = routed_scale * quant / jnp.sum(quant, axis=1, keepdims=True)
    n_rows = rows_in.shape[0]
    for s in range(n_slots):
        mine = jnp.where(named == slots[s].astype(f32), gates, 0.0)
        column = jnp.sum(mine, axis=1, keepdims=True)
        scale[s] = jnp.broadcast_to(column, (n_rows, lanes))

    def silu(v):
        return v / (1.0 + jnp.exp(-v))

    for i in range(n_slots * tiles):
        if i == 2:
            arrived(shared_copy)
            both = jnp.dot(rows_in[:, :model_dim], shared_w[...], preferred_element_type=f32)
            shared_act = (silu(both[:, :sp]) * both[:, sp:]).astype(bf16)
            act[:, experts_k : experts_k + sp] = shared_act
        for copy in gu_copies[2 * i : 2 * i + 2]:
            arrived(copy)
        g = jnp.dot(rows_in[:, :model_dim], wgu[i, 0], preferred_element_type=f32)
        u = jnp.dot(rows_in[:, :model_dim], wgu[i, 1], preferred_element_type=f32)
        by = jnp.concatenate([scale[i // tiles]] * (hid_tile // lanes), axis=1)
        act[:, i * hid_tile : (i + 1) * hid_tile] = (silu(g) * u * by).astype(bf16)

    level_rows = ny * tok_rows
    for h, n, group in dn_copies:
        for copy in group:
            arrived(copy)
        columns = pl.ds(*cuts[n])
        value = jnp.dot(act[...], wdn[h, :, columns], preferred_element_type=f32).astype(bf16)
        if x_first is None:
            for i in range(len(levels)):
                for j in range(ny):
                    base = i * level_rows + j * tok_rows
                    outs[j][h][i, :, columns] = value[base : base + tok_rows]
            continue
        for i in range(len(levels)):
            if x_first[i]:
                outs[i][h][:, columns] = value[i * level_rows : (i + 1) * level_rows]
            else:
                for j in range(ny):
                    base = i * level_rows + j * tok_rows
                    outs[i][j][h, :, columns] = value[base : base + tok_rows]


def local(
    tokens, routes, gate_quant, swap_codes, expert_gate_up, expert_down, shared_gate_up, shared_down
):
    axis_width = lax.axis_size("expert")
    nx = lax.axis_size("dp")
    ny = nx
    nz = axis_width // (2 * ny)
    zs = 2 * ny
    per_device, hidden, model_dim = expert_down.shape
    tok_rows = tokens.shape[0]
    top_count = routes.shape[1]
    me = lax.axis_index("expert")
    mx = lax.axis_index("dp")
    part = tok_rows // nx
    width = model_dim // nx
    hid_tile = 256 if hidden % 256 == 0 else 128

    pad = -3 * top_count % lanes
    wide = jnp.concatenate(
        [
            tokens,
            routes.astype(bf16),
            (gate_quant // 256).astype(bf16),
            (gate_quant % 256).astype(bf16),
            jnp.zeros((tok_rows, pad), bf16),
        ],
        axis=1,
    )
    wide_dim = wide.shape[1]

    gu_sib = hop(expert_gate_up, 1)
    dn_sib = hop(expert_down, 1)
    shared_rows = shared_down.shape[0]
    shared_own = jnp.concatenate(
        [shared_gate_up[:, 0, :], shared_gate_up[:, 1, :], shared_down], axis=0
    )
    shared_both = jnp.stack([shared_own, hop(shared_own, 1)])
    shared_both = shared_both.reshape(2, 3, shared_rows, model_dim).transpose(1, 0, 2, 3)
    shared_both = shared_both.reshape(3, 2 * shared_rows, model_dim)
    shared_both = jnp.pad(shared_both, ((0, 0), (0, -2 * shared_rows % 16), (0, 0)))
    sp = shared_both.shape[1]
    sh_gu = shared_both[:2].reshape(2 * sp, model_dim).T
    sh_dn = shared_both[2]

    my_experts = jnp.concatenate(
        [owner * per_device + jnp.arange(per_device, dtype=jnp.int32) for owner in (me, me ^ 1)]
    )
    slots = remapped(my_experts, swap_codes, per_device, axis_width // 2)

    half = nz // 2
    held = lax.dynamic_slice_in_dim(wide, mx * part, part, axis=0)
    own = [wide] + [hop(wide, 2 * j) for j in range(1, ny)]
    bits = [0]
    step = half
    while step > 1:
        held = jnp.concatenate([held, hop(held, step * zs)], axis=0)
        bits = bits + [bit ^ step for bit in bits]
        step //= 2
    far = hop(held, zs)
    bits = bits + [bit ^ 1 for bit in bits]

    def spread(x):
        return [[hop(x, 2 * j, h) if j or h else x for h in range(nx)] for j in range(ny)]

    near_units = spread(lax.optimization_barrier([held[part:]] + own[1:])[0])
    near = [u for j in range(ny) for u in near_units[j]]
    far = lax.optimization_barrier([far] + near)[0]
    far_units = spread(far)
    chunks = [
        [u for j in range(ny) for u in [own[j]] + near_units[j]],
        [u for j in range(ny) for u in far_units[j]],
    ]

    def added(own, others):
        total = own.astype(f32)
        for other in others:
            total = total + other.astype(f32)
        return total

    done = {}
    n_slots = 2 * per_device
    tiles = hidden // hid_tile
    after = []
    for levels in (list(range(half)), list(range(half, nz))):
        x_first = [k % 2 == 1 for k in levels] if levels[0] else None
        chunk = chunks[levels[0] // half]
        n_rows = len(levels) * ny * tok_rows
        out_shape = []
        if x_first is None:
            shape = (len(levels), tok_rows, width)
            out_shape = [jax.ShapeDtypeStruct(shape, bf16)] * (ny * nx)
        for first in x_first or []:
            shape = (ny * tok_rows, width) if first else (nx, tok_rows, width)
            out_shape += [jax.ShapeDtypeStruct(shape, bf16)] * nx
        k_total = n_slots * hidden + sp
        flops = 2 * n_rows * model_dim * (3 * n_slots * hidden + 3 * sp)
        outs = pl.pallas_call(
            functools.partial(
                ffn_kernel,
                levels,
                x_first,
                nx,
                ny,
                tok_rows,
                top_count,
                model_dim,
                hid_tile,
                len(chunk),
                len(after),
            ),
            out_shape=out_shape,
            in_specs=[pl.BlockSpec(memory_space=pltpu.SMEM)]
            + [pl.BlockSpec(memory_space=pl.ANY)] * (len(chunk) + 6 + len(after)),
            out_specs=[pl.BlockSpec(memory_space=pltpu.VMEM)] * len(out_shape),
            scratch_shapes=[
                pltpu.VMEM((n_rows, wide_dim), bf16),
                pltpu.VMEM((model_dim, 2 * sp), bf16),
                pltpu.VMEM((n_slots * tiles, 2, model_dim, hid_tile), bf16),
                pltpu.VMEM((nx, k_total, width), bf16),
                pltpu.VMEM((n_rows, k_total), bf16),
                pltpu.VMEM((n_slots, n_rows, lanes), f32),
                pltpu.SemaphoreType.DMA((len(levels) * ny * nx,)),
                pltpu.SemaphoreType.DMA((1,)),
                pltpu.SemaphoreType.DMA((n_slots * tiles, 2)),
                pltpu.SemaphoreType.DMA((nx, -(-width // cut), n_slots + 1)),
            ],
            compiler_params=pltpu.CompilerParams(vmem_limit_bytes=60 * 1024 * 1024),
            cost_estimate=pl.CostEstimate(
                flops=flops,
                bytes_accessed=3 * 2 * n_slots * hidden * model_dim + 6 * n_rows * model_dim,
                transcendentals=0,
            ),
        )(slots, *chunk, sh_gu, sh_dn, expert_gate_up, gu_sib, expert_down, dn_sib, *after)
        after = outs[:1]
        if x_first is None:
            got = [
                hop(outs[j * nx + h], 2 * j, h) for j in range(ny) for h in range(nx) if j or h
            ]
            planes = added(outs[0], got)
            early = got
            for i, k in enumerate(levels):
                done[k] = planes[i] if k == 0 else hop(planes[i].astype(bf16), bits[k] * zs)
            continue
        outs = lax.optimization_barrier(list(outs) + early)[: len(outs)]
        for i, k in enumerate(levels):
            sent = outs[i * nx : (i + 1) * nx]
            if x_first[i]:
                got = [hop(sent[h], 0, h) for h in range(1, nx)]
                row = added(sent[0], got).astype(bf16).reshape(ny, tok_rows, width)
                got = [hop(row[j], 2 * j) for j in range(1, ny)]
            else:
                got = [hop(sent[j], 2 * j) for j in range(1, ny)]
                row = added(sent[0], got).astype(bf16)
                got = [hop(row[h], 0, h) for h in range(1, nx)]
            plane = added(row[0], got)
            done[k] = plane if k == 0 else hop(plane.astype(bf16), bits[k] * zs)
    return added(done[0], [done[k] for k in range(1, nz)]).astype(bf16)


def solution(mesh):
    in_specs = (
        P("expert", None),
        P("expert", None),
        P("expert", None),
        P(),
        P("expert", None, None, "dp"),
        P("expert", "dp", None),
        P(("dp", "expert"), None, None),
        P(("dp", "expert"), None),
    )
    out_specs = P("expert", "dp")
    return jax.shard_map(local, mesh=mesh, in_specs=in_specs, out_specs=out_specs, check_vma=False)
```

```python
import functools

import jax
import jax.numpy as jnp
from jax import lax
from jax.experimental import pallas as pl
from jax.experimental.pallas import tpu as pltpu
from jax.sharding import PartitionSpec as P

routed_scale = 2.5
lanes = 128
in_flight = 6
cut = 2048
f32 = jnp.float32
bf16 = jnp.bfloat16


def remapped(routes, swap_codes, per_device, half_width):
    owner = routes // per_device
    slot = routes % per_device
    pair_ids = jnp.arange(half_width, dtype=jnp.int32)
    code = jnp.sum(
        jnp.where((owner % half_width)[..., None] == pair_ids, swap_codes, 0), axis=-1
    )
    lower = owner < half_width
    low_slot = (code - 1) // per_device
    high_slot = (code - 1) % per_device
    traded = (code > 0) & (slot == jnp.where(lower, low_slot, high_slot))
    partner = jnp.where(
        lower,
        (owner + half_width) * per_device + high_slot,
        (owner - half_width) * per_device + low_slot,
    )
    return jnp.where(traded, partner, routes)


def hop(x, by, by_x=0):
    ne = lax.axis_size("expert")
    count = ne * lax.axis_size("dp")
    return lax.ppermute(x, ("dp", "expert"), [(i, i ^ (by_x * ne + by)) for i in range(count)])


def ffn_kernel(
    levels, x_first, nx, ny, tok_rows, top_count, model_dim, hid_tile, n_units, n_after, *refs
):
    slots = refs[0]
    units = refs[1 : 1 + n_units]
    sh_gu, sh_dn, gu_own, gu_sib, dn_own, dn_sib = refs[1 + n_units : 7 + n_units]
    refs = refs[7 + n_units + n_after :]
    groups = ny if x_first is None else len(levels)
    outs = [refs[i * nx : (i + 1) * nx] for i in range(groups)]
    rows_in, shared_w, wgu, wdn, act, scale, sem_x, sem_s, sem_gu, sem_dn = refs[groups * nx :]
    mx = lax.axis_index("dp")
    part = tok_rows // nx
    width = model_dim // nx
    per_device, _, _, hidden = gu_own.shape
    tiles = hidden // hid_tile
    n_slots = 2 * per_device
    experts_k = n_slots * hidden
    sp = sh_dn.shape[0]

    copies = []

    def take(unit, start, size, row):
        dst = rows_in.at[pl.ds(row, size)]
        copies.append(
            pltpu.make_async_copy(unit.at[pl.ds(start, size)], dst, sem_x.at[len(copies)])
        )

    at = 0
    for j in range(ny):
        if levels[0] == 0:
            take(units[at], 0, tok_rows, j * tok_rows)
            at += 1
        for h in range(nx):
            for n, i in enumerate(i for i in range(len(levels)) if levels[i]):
                row = (i * ny + j) * tok_rows + (mx ^ h) * part
                take(units[at], n * part, part, pl.multiple_of(row, part))
            at += 1
    shared_copy = pltpu.make_async_copy(sh_gu, shared_w, sem_s.at[0])

    def gu_copy(src, e, t, i, g):
        return pltpu.make_async_copy(
            src.at[e, g, :, pl.ds(t * hid_tile, hid_tile)], wgu.at[i, g], sem_gu.at[i, g]
        )

    cuts = [(at, min(cut, width - at)) for at in range(0, width, cut)]

    def dn_copy(src, e, h, s, n):
        at, size = cuts[n]
        column = pl.multiple_of((mx ^ h) * width + at, lanes)
        return pltpu.make_async_copy(
            src.at[e, :, pl.ds(column, size)],
            wdn.at[h, pl.ds(s * hidden, hidden), pl.ds(at, size)],
            sem_dn.at[h, n, s],
        )

    def sh_copy(h, n):
        at, size = cuts[n]
        column = pl.multiple_of((mx ^ h) * width + at, lanes)
        return pltpu.make_async_copy(
            sh_dn.at[:, pl.ds(column, size)],
            wdn.at[h, pl.ds(experts_k, sp), pl.ds(at, size)],
            sem_dn.at[h, n, n_slots],
        )

    order = list(range(1, nx)) + [0]
    gu_copies = []
    for s in range(n_slots):
        src = gu_own if s < per_device else gu_sib
        for t in range(tiles):
            for g in range(2):
                gu_copies.append(gu_copy(src, s % per_device, t, s * tiles + t, g))
    dn_copies = []
    for h in order:
        for n in range(len(cuts)):
            group = [sh_copy(h, n)]
            for s in range(n_slots):
                src = dn_own if s < per_device else dn_sib
                group.append(dn_copy(src, s % per_device, h, s, n))
            dn_copies.append((h, n, group))

    queue = gu_copies[:4] + [shared_copy] + gu_copies[4:]
    queue += [copy for _, _, group in dn_copies for copy in group]
    started = [0]

    def start_next(count):
        for copy in queue[started[0] : started[0] + count]:
            copy.start()
        started[0] += count

    def arrived(copy):
        copy.wait()
        start_next(1)

    for copy in copies:
        copy.start()
    start_next(in_flight)
    for copy in copies:
        copy.wait()
    extra = rows_in[:, model_dim:].astype(f32)
    named = extra[:, :top_count]
    quant = extra[:, top_count : 2 * top_count] * 256.0 + extra[:, 2 * top_count : 3 * top_count]
    gates = routed_scale * quant / jnp.sum(quant, axis=1, keepdims=True)
    n_rows = rows_in.shape[0]
    for s in range(n_slots):
        mine = jnp.where(named == slots[s].astype(f32), gates, 0.0)
        column = jnp.sum(mine, axis=1, keepdims=True)
        scale[s] = jnp.broadcast_to(column, (n_rows, lanes))

    def silu(v):
        return v / (1.0 + jnp.exp(-v))

    for i in range(n_slots * tiles):
        if i == 2:
            arrived(shared_copy)
            both = jnp.dot(rows_in[:, :model_dim], shared_w[...], preferred_element_type=f32)
            shared_act = (silu(both[:, :sp]) * both[:, sp:]).astype(bf16)
            act[:, experts_k : experts_k + sp] = shared_act
        for copy in gu_copies[2 * i : 2 * i + 2]:
            arrived(copy)
        g = jnp.dot(rows_in[:, :model_dim], wgu[i, 0], preferred_element_type=f32)
        u = jnp.dot(rows_in[:, :model_dim], wgu[i, 1], preferred_element_type=f32)
        by = jnp.concatenate([scale[i // tiles]] * (hid_tile // lanes), axis=1)
        act[:, i * hid_tile : (i + 1) * hid_tile] = (silu(g) * u * by).astype(bf16)

    level_rows = ny * tok_rows
    for h, n, group in dn_copies:
        for copy in group:
            arrived(copy)
        columns = pl.ds(*cuts[n])
        value = jnp.dot(act[...], wdn[h, :, columns], preferred_element_type=f32).astype(bf16)
        if x_first is None:
            for i in range(len(levels)):
                for j in range(ny):
                    base = i * level_rows + j * tok_rows
                    outs[j][h][i, :, columns] = value[base : base + tok_rows]
            continue
        for i in range(len(levels)):
            if x_first[i]:
                outs[i][h][:, columns] = value[i * level_rows : (i + 1) * level_rows]
            else:
                for j in range(ny):
                    base = i * level_rows + j * tok_rows
                    outs[i][j][h, :, columns] = value[base : base + tok_rows]


def local(
    tokens, routes, gate_quant, swap_codes, expert_gate_up, expert_down, shared_gate_up, shared_down
):
    axis_width = lax.axis_size("expert")
    nx = lax.axis_size("dp")
    ny = nx
    nz = axis_width // (2 * ny)
    zs = 2 * ny
    per_device, hidden, model_dim = expert_down.shape
    tok_rows = tokens.shape[0]
    top_count = routes.shape[1]
    me = lax.axis_index("expert")
    mx = lax.axis_index("dp")
    part = tok_rows // nx
    width = model_dim // nx
    hid_tile = 256 if hidden % 256 == 0 else 128

    pad = -3 * top_count % lanes
    wide = jnp.concatenate(
        [
            tokens,
            routes.astype(bf16),
            (gate_quant // 256).astype(bf16),
            (gate_quant % 256).astype(bf16),
            jnp.zeros((tok_rows, pad), bf16),
        ],
        axis=1,
    )
    wide_dim = wide.shape[1]

    gu_sib = hop(expert_gate_up, 1)
    dn_sib = hop(expert_down, 1)
    shared_rows = shared_down.shape[0]
    shared_own = jnp.concatenate(
        [shared_gate_up[:, 0, :], shared_gate_up[:, 1, :], shared_down], axis=0
    )
    shared_both = jnp.stack([shared_own, hop(shared_own, 1)])
    shared_both = shared_both.reshape(2, 3, shared_rows, model_dim).transpose(1, 0, 2, 3)
    shared_both = shared_both.reshape(3, 2 * shared_rows, model_dim)
    shared_both = jnp.pad(shared_both, ((0, 0), (0, -2 * shared_rows % 16), (0, 0)))
    sp = shared_both.shape[1]
    sh_gu = shared_both[:2].reshape(2 * sp, model_dim).T
    sh_dn = shared_both[2]

    my_experts = jnp.concatenate(
        [owner * per_device + jnp.arange(per_device, dtype=jnp.int32) for owner in (me, me ^ 1)]
    )
    slots = remapped(my_experts, swap_codes, per_device, axis_width // 2)

    half = nz // 2
    held = lax.dynamic_slice_in_dim(wide, mx * part, part, axis=0)
    own = [wide] + [hop(lax.optimization_barrier((wide, held))[0], 2 * j) for j in range(1, ny)]
    bits = [0]
    step = half
    while step > 1:
        held = jnp.concatenate([held, hop(held, step * zs)], axis=0)
        bits = bits + [bit ^ step for bit in bits]
        step //= 2
    far = hop(held, zs)
    bits = bits + [bit ^ 1 for bit in bits]

    def spread(x):
        return [[hop(x, 2 * j, h) if j or h else x for h in range(nx)] for j in range(ny)]

    near_units = spread(lax.optimization_barrier([held[part:]] + own[1:])[0])
    near = [u for j in range(ny) for u in near_units[j]]
    far = lax.optimization_barrier([far, near[1]])[0]
    far_units = spread(far)
    chunks = [
        [u for j in range(ny) for u in [own[j]] + near_units[j]],
        [u for j in range(ny) for u in far_units[j]],
    ]

    def added(own, others):
        total = own.astype(f32)
        for other in others:
            total = total + other.astype(f32)
        return total

    done = {}
    n_slots = 2 * per_device
    tiles = hidden // hid_tile
    after = []
    for levels in (list(range(half)), list(range(half, nz))):
        x_first = [k % 2 == 0 for k in levels] if levels[0] else None
        chunk = chunks[levels[0] // half]
        n_rows = len(levels) * ny * tok_rows
        out_shape = []
        if x_first is None:
            shape = (len(levels), tok_rows, width)
            out_shape = [jax.ShapeDtypeStruct(shape, bf16)] * (ny * nx)
        for first in x_first or []:
            shape = (ny * tok_rows, width) if first else (nx, tok_rows, width)
            out_shape += [jax.ShapeDtypeStruct(shape, bf16)] * nx
        k_total = n_slots * hidden + sp
        flops = 2 * n_rows * model_dim * (3 * n_slots * hidden + 3 * sp)
        outs = pl.pallas_call(
            functools.partial(
                ffn_kernel,
                levels,
                x_first,
                nx,
                ny,
                tok_rows,
                top_count,
                model_dim,
                hid_tile,
                len(chunk),
                len(after),
            ),
            out_shape=out_shape,
            in_specs=[pl.BlockSpec(memory_space=pltpu.SMEM)]
            + [pl.BlockSpec(memory_space=pl.ANY)] * (len(chunk) + 6 + len(after)),
            out_specs=[pl.BlockSpec(memory_space=pltpu.VMEM)] * len(out_shape),
            scratch_shapes=[
                pltpu.VMEM((n_rows, wide_dim), bf16),
                pltpu.VMEM((model_dim, 2 * sp), bf16),
                pltpu.VMEM((n_slots * tiles, 2, model_dim, hid_tile), bf16),
                pltpu.VMEM((nx, k_total, width), bf16),
                pltpu.VMEM((n_rows, k_total), bf16),
                pltpu.VMEM((n_slots, n_rows, lanes), f32),
                pltpu.SemaphoreType.DMA((len(levels) * ny * nx,)),
                pltpu.SemaphoreType.DMA((1,)),
                pltpu.SemaphoreType.DMA((n_slots * tiles, 2)),
                pltpu.SemaphoreType.DMA((nx, -(-width // cut), n_slots + 1)),
            ],
            compiler_params=pltpu.CompilerParams(vmem_limit_bytes=60 * 1024 * 1024),
            cost_estimate=pl.CostEstimate(
                flops=flops,
                bytes_accessed=3 * 2 * n_slots * hidden * model_dim + 6 * n_rows * model_dim,
                transcendentals=0,
            ),
        )(slots, *chunk, sh_gu, sh_dn, expert_gate_up, gu_sib, expert_down, dn_sib, *after)
        after = outs[:1]
        if x_first is None:
            got = [
                hop(outs[j * nx + h], 2 * j, h) for j in range(ny) for h in range(nx) if j or h
            ]
            planes = added(outs[0], got)
            early = got
            for i, k in enumerate(levels):
                done[k] = planes[i] if k == 0 else hop(planes[i].astype(bf16), bits[k] * zs)
            continue
        outs = lax.optimization_barrier(list(outs) + early)[: len(outs)]
        for i, k in enumerate(levels):
            sent = outs[i * nx : (i + 1) * nx]
            if x_first[i]:
                got = [hop(sent[h], 0, h) for h in range(1, nx)]
                row = added(sent[0], got).astype(bf16).reshape(ny, tok_rows, width)
                got = [hop(row[j], 2 * j) for j in range(1, ny)]
            else:
                got = [hop(sent[j], 2 * j) for j in range(1, ny)]
                row = added(sent[0], got).astype(bf16)
                got = [hop(row[h], 0, h) for h in range(1, nx)]
            plane = added(row[0], got)
            done[k] = plane if k == 0 else hop(plane.astype(bf16), bits[k] * zs)
    return added(done[0], [done[k] for k in range(1, nz)]).astype(bf16)


def solution(mesh):
    in_specs = (
        P("expert", None),
        P("expert", None),
        P("expert", None),
        P(),
        P("expert", None, None, "dp"),
        P("expert", "dp", None),
        P(("dp", "expert"), None, None),
        P(("dp", "expert"), None),
    )
    out_specs = P("expert", "dp")
    return jax.shard_map(local, mesh=mesh, in_specs=in_specs, out_specs=out_specs, check_vma=False)
```

```python
import functools

import jax
import jax.numpy as jnp
from jax import lax
from jax.experimental import pallas as pl
from jax.experimental.pallas import tpu as pltpu
from jax.sharding import PartitionSpec as P

routed_scale = 2.5
lanes = 128
in_flight = 6
cut = 2048
f32 = jnp.float32
bf16 = jnp.bfloat16


def remapped(routes, swap_codes, per_device, half_width):
    owner = routes // per_device
    slot = routes % per_device
    pair_ids = jnp.arange(half_width, dtype=jnp.int32)
    code = jnp.sum(
        jnp.where((owner % half_width)[..., None] == pair_ids, swap_codes, 0), axis=-1
    )
    lower = owner < half_width
    low_slot = (code - 1) // per_device
    high_slot = (code - 1) % per_device
    traded = (code > 0) & (slot == jnp.where(lower, low_slot, high_slot))
    partner = jnp.where(
        lower,
        (owner + half_width) * per_device + high_slot,
        (owner - half_width) * per_device + low_slot,
    )
    return jnp.where(traded, partner, routes)


def hop(x, by, by_x=0):
    ne = lax.axis_size("expert")
    count = ne * lax.axis_size("dp")
    return lax.ppermute(x, ("dp", "expert"), [(i, i ^ (by_x * ne + by)) for i in range(count)])


def ffn_kernel(
    levels, x_first, nx, ny, tok_rows, top_count, model_dim, hid_tile, n_units, n_after, *refs
):
    slots = refs[0]
    units = refs[1 : 1 + n_units]
    sh_gu, sh_dn, gu_own, gu_sib, dn_own, dn_sib = refs[1 + n_units : 7 + n_units]
    refs = refs[7 + n_units + n_after :]
    groups = ny if x_first is None else len(levels)
    outs = [refs[i * nx : (i + 1) * nx] for i in range(groups)]
    rows_in, shared_w, wgu, wdn, act, scale, sem_x, sem_s, sem_gu, sem_dn = refs[groups * nx :]
    mx = lax.axis_index("dp")
    part = tok_rows // nx
    width = model_dim // nx
    per_device, _, _, hidden = gu_own.shape
    tiles = hidden // hid_tile
    n_slots = 2 * per_device
    experts_k = n_slots * hidden
    sp = sh_dn.shape[0]

    copies = []

    def take(unit, start, size, row):
        dst = rows_in.at[pl.ds(row, size)]
        copies.append(
            pltpu.make_async_copy(unit.at[pl.ds(start, size)], dst, sem_x.at[len(copies)])
        )

    at = 0
    for j in range(ny):
        if levels[0] == 0:
            take(units[at], 0, tok_rows, j * tok_rows)
            at += 1
        for h in range(nx):
            for n, i in enumerate(i for i in range(len(levels)) if levels[i]):
                row = (i * ny + j) * tok_rows + (mx ^ h) * part
                take(units[at], n * part, part, pl.multiple_of(row, part))
            at += 1
    shared_copy = pltpu.make_async_copy(sh_gu, shared_w, sem_s.at[0])

    def gu_copy(src, e, t, i, g):
        return pltpu.make_async_copy(
            src.at[e, g, :, pl.ds(t * hid_tile, hid_tile)], wgu.at[i, g], sem_gu.at[i, g]
        )

    cuts = [(at, min(cut, width - at)) for at in range(0, width, cut)]

    def dn_copy(src, e, h, s, n):
        at, size = cuts[n]
        column = pl.multiple_of((mx ^ h) * width + at, lanes)
        return pltpu.make_async_copy(
            src.at[e, :, pl.ds(column, size)],
            wdn.at[h, pl.ds(s * hidden, hidden), pl.ds(at, size)],
            sem_dn.at[h, n, s],
        )

    def sh_copy(h, n):
        at, size = cuts[n]
        column = pl.multiple_of((mx ^ h) * width + at, lanes)
        return pltpu.make_async_copy(
            sh_dn.at[:, pl.ds(column, size)],
            wdn.at[h, pl.ds(experts_k, sp), pl.ds(at, size)],
            sem_dn.at[h, n, n_slots],
        )

    order = list(range(1, nx)) + [0]
    gu_copies = []
    for s in range(n_slots):
        src = gu_own if s < per_device else gu_sib
        for t in range(tiles):
            for g in range(2):
                gu_copies.append(gu_copy(src, s % per_device, t, s * tiles + t, g))
    dn_copies = []
    for h in order:
        for n in range(len(cuts)):
            group = [sh_copy(h, n)]
            for s in range(n_slots):
                src = dn_own if s < per_device else dn_sib
                group.append(dn_copy(src, s % per_device, h, s, n))
            dn_copies.append((h, n, group))

    queue = gu_copies[:4] + [shared_copy] + gu_copies[4:]
    queue += [copy for _, _, group in dn_copies for copy in group]
    started = [0]

    def start_next(count):
        for copy in queue[started[0] : started[0] + count]:
            copy.start()
        started[0] += count

    def arrived(copy):
        copy.wait()
        start_next(1)

    for copy in copies:
        copy.start()
    start_next(in_flight)
    for copy in copies:
        copy.wait()
    extra = rows_in[:, model_dim:].astype(f32)
    named = extra[:, :top_count]
    quant = extra[:, top_count : 2 * top_count] * 256.0 + extra[:, 2 * top_count : 3 * top_count]
    gates = routed_scale * quant / jnp.sum(quant, axis=1, keepdims=True)
    n_rows = rows_in.shape[0]
    for s in range(n_slots):
        mine = jnp.where(named == slots[s].astype(f32), gates, 0.0)
        column = jnp.sum(mine, axis=1, keepdims=True)
        scale[s] = jnp.broadcast_to(column, (n_rows, lanes))

    def silu(v):
        return v / (1.0 + jnp.exp(-v))

    for i in range(n_slots * tiles):
        if i == 2:
            arrived(shared_copy)
            both = jnp.dot(rows_in[:, :model_dim], shared_w[...], preferred_element_type=f32)
            shared_act = (silu(both[:, :sp]) * both[:, sp:]).astype(bf16)
            act[:, experts_k : experts_k + sp] = shared_act
        for copy in gu_copies[2 * i : 2 * i + 2]:
            arrived(copy)
        g = jnp.dot(rows_in[:, :model_dim], wgu[i, 0], preferred_element_type=f32)
        u = jnp.dot(rows_in[:, :model_dim], wgu[i, 1], preferred_element_type=f32)
        by = jnp.concatenate([scale[i // tiles]] * (hid_tile // lanes), axis=1)
        act[:, i * hid_tile : (i + 1) * hid_tile] = (silu(g) * u * by).astype(bf16)

    level_rows = ny * tok_rows
    for h, n, group in dn_copies:
        for copy in group:
            arrived(copy)
        columns = pl.ds(*cuts[n])
        value = jnp.dot(act[...], wdn[h, :, columns], preferred_element_type=f32).astype(bf16)
        if x_first is None:
            for i in range(len(levels)):
                for j in range(ny):
                    base = i * level_rows + j * tok_rows
                    outs[j][h][i, :, columns] = value[base : base + tok_rows]
            continue
        for i in range(len(levels)):
            if x_first[i]:
                outs[i][h][:, columns] = value[i * level_rows : (i + 1) * level_rows]
            else:
                for j in range(ny):
                    base = i * level_rows + j * tok_rows
                    outs[i][j][h, :, columns] = value[base : base + tok_rows]


def local(
    tokens, routes, gate_quant, swap_codes, expert_gate_up, expert_down, shared_gate_up, shared_down
):
    axis_width = lax.axis_size("expert")
    nx = lax.axis_size("dp")
    ny = nx
    nz = axis_width // (2 * ny)
    zs = 2 * ny
    per_device, hidden, model_dim = expert_down.shape
    tok_rows = tokens.shape[0]
    top_count = routes.shape[1]
    me = lax.axis_index("expert")
    mx = lax.axis_index("dp")
    part = tok_rows // nx
    width = model_dim // nx
    hid_tile = 256 if hidden % 256 == 0 else 128

    pad = -3 * top_count % lanes
    wide = jnp.concatenate(
        [
            tokens,
            routes.astype(bf16),
            (gate_quant // 256).astype(bf16),
            (gate_quant % 256).astype(bf16),
            jnp.zeros((tok_rows, pad), bf16),
        ],
        axis=1,
    )
    wide_dim = wide.shape[1]

    gu_sib = hop(expert_gate_up, 1)
    dn_sib = hop(expert_down, 1)
    shared_rows = shared_down.shape[0]
    shared_own = jnp.concatenate(
        [shared_gate_up[:, 0, :], shared_gate_up[:, 1, :], shared_down], axis=0
    )
    shared_both = jnp.stack([shared_own, hop(shared_own, 1)])
    shared_both = shared_both.reshape(2, 3, shared_rows, model_dim).transpose(1, 0, 2, 3)
    shared_both = shared_both.reshape(3, 2 * shared_rows, model_dim)
    shared_both = jnp.pad(shared_both, ((0, 0), (0, -2 * shared_rows % 16), (0, 0)))
    sp = shared_both.shape[1]
    sh_gu = shared_both[:2].reshape(2 * sp, model_dim).T
    sh_dn = shared_both[2]

    my_experts = jnp.concatenate(
        [owner * per_device + jnp.arange(per_device, dtype=jnp.int32) for owner in (me, me ^ 1)]
    )
    slots = remapped(my_experts, swap_codes, per_device, axis_width // 2)

    half = nz // 2
    held = lax.dynamic_slice_in_dim(wide, mx * part, part, axis=0)
    own = [wide] + [hop(lax.optimization_barrier((wide, held))[0], 2 * j) for j in range(1, ny)]
    bits = [0]
    step = half
    while step > 1:
        held = jnp.concatenate([held, hop(held, step * zs)], axis=0)
        bits = bits + [bit ^ step for bit in bits]
        step //= 2
    far = hop(held, zs)
    bits = bits + [bit ^ 1 for bit in bits]

    def spread(x):
        return [[hop(x, 2 * j, h) if j or h else x for h in range(nx)] for j in range(ny)]

    near_units = spread(lax.optimization_barrier([held[part:]] + own[1:])[0])
    far_units = spread(far)
    chunks = [
        [u for j in range(ny) for u in [own[j]] + near_units[j]],
        [u for j in range(ny) for u in far_units[j]],
    ]

    def added(own, others):
        total = own.astype(f32)
        for other in others:
            total = total + other.astype(f32)
        return total

    done = {}
    n_slots = 2 * per_device
    tiles = hidden // hid_tile
    after = []
    for levels in (list(range(half)), list(range(half, nz))):
        x_first = [k % 2 == 0 for k in levels] if levels[0] else None
        chunk = chunks[levels[0] // half]
        n_rows = len(levels) * ny * tok_rows
        out_shape = []
        if x_first is None:
            shape = (len(levels), tok_rows, width)
            out_shape = [jax.ShapeDtypeStruct(shape, bf16)] * (ny * nx)
        for first in x_first or []:
            shape = (ny * tok_rows, width) if first else (nx, tok_rows, width)
            out_shape += [jax.ShapeDtypeStruct(shape, bf16)] * nx
        k_total = n_slots * hidden + sp
        flops = 2 * n_rows * model_dim * (3 * n_slots * hidden + 3 * sp)
        outs = pl.pallas_call(
            functools.partial(
                ffn_kernel,
                levels,
                x_first,
                nx,
                ny,
                tok_rows,
                top_count,
                model_dim,
                hid_tile,
                len(chunk),
                len(after),
            ),
            out_shape=out_shape,
            in_specs=[pl.BlockSpec(memory_space=pltpu.SMEM)]
            + [pl.BlockSpec(memory_space=pl.ANY)] * (len(chunk) + 6 + len(after)),
            out_specs=[pl.BlockSpec(memory_space=pltpu.VMEM)] * len(out_shape),
            scratch_shapes=[
                pltpu.VMEM((n_rows, wide_dim), bf16),
                pltpu.VMEM((model_dim, 2 * sp), bf16),
                pltpu.VMEM((n_slots * tiles, 2, model_dim, hid_tile), bf16),
                pltpu.VMEM((nx, k_total, width), bf16),
                pltpu.VMEM((n_rows, k_total), bf16),
                pltpu.VMEM((n_slots, n_rows, lanes), f32),
                pltpu.SemaphoreType.DMA((len(levels) * ny * nx,)),
                pltpu.SemaphoreType.DMA((1,)),
                pltpu.SemaphoreType.DMA((n_slots * tiles, 2)),
                pltpu.SemaphoreType.DMA((nx, -(-width // cut), n_slots + 1)),
            ],
            compiler_params=pltpu.CompilerParams(vmem_limit_bytes=60 * 1024 * 1024),
            cost_estimate=pl.CostEstimate(
                flops=flops,
                bytes_accessed=3 * 2 * n_slots * hidden * model_dim + 6 * n_rows * model_dim,
                transcendentals=0,
            ),
        )(slots, *chunk, sh_gu, sh_dn, expert_gate_up, gu_sib, expert_down, dn_sib, *after)
        after = outs[:1]
        if x_first is None:
            got = [
                hop(outs[j * nx + h], 2 * j, h) for j in range(ny) for h in range(nx) if j or h
            ]
            planes = added(outs[0], got)
            early = got
            for i, k in enumerate(levels):
                done[k] = planes[i] if k == 0 else hop(planes[i].astype(bf16), bits[k] * zs)
            continue
        outs = lax.optimization_barrier(list(outs) + early)[: len(outs)]
        for i, k in enumerate(levels):
            sent = outs[i * nx : (i + 1) * nx]
            if x_first[i]:
                got = [hop(sent[h], 0, h) for h in range(1, nx)]
                row = added(sent[0], got).astype(bf16).reshape(ny, tok_rows, width)
                got = [hop(row[j], 2 * j) for j in range(1, ny)]
            else:
                got = [hop(sent[j], 2 * j) for j in range(1, ny)]
                row = added(sent[0], got).astype(bf16)
                got = [hop(row[h], 0, h) for h in range(1, nx)]
            plane = added(row[0], got)
            done[k] = plane if k == 0 else hop(plane.astype(bf16), bits[k] * zs)
    return added(done[0], [done[k] for k in range(1, nz)]).astype(bf16)


def solution(mesh):
    in_specs = (
        P("expert", None),
        P("expert", None),
        P("expert", None),
        P(),
        P("expert", None, None, "dp"),
        P("expert", "dp", None),
        P(("dp", "expert"), None, None),
        P(("dp", "expert"), None),
    )
    out_specs = P("expert", "dp")
    return jax.shard_map(local, mesh=mesh, in_specs=in_specs, out_specs=out_specs, check_vma=False)
```
